512 devices in a mesh: dp: 16 (over z, core), tp: 32 (over y, x).
Axes of the slice: x: 4, y: 8, z: 8, core: 2. Of those that a mesh axis runs over, the one named last changes fastest.
Arguments:
- queries: bfloat16 [1024, 128, 576], P(('dp', 'tp')), may hold values from -95 to 95
- latent_cache: bfloat16 [1024, 1024, 576], P(('dp', 'tp')), may hold values from -4 to 4
- lengths: int32 [1024], P(('dp', 'tp')), may hold values from 2 to 1024, as said below
- counts: int32 [512], P(('dp', 'tp')), may hold values from 1 to 2, as said below
- value_up: bfloat16 [128, 512, 128], P('tp'), may hold values from -4 to 4
- out_proj: bfloat16 [16384, 7168], P('tp', 'dp'), may hold values from -0.25 to 0.25
- residual: bfloat16 [1024, 7168], P('tp', 'dp'), may hold values from -6 to 6
Outputs:
- layer_out: bfloat16 [1024, 7168], P('tp', 'dp')
The draws below stay inside these ranges and needn't reach their ends.
Inputs may be any that keep to these rules, and one draw needn't show every extreme that they name: `counts`: slots 0 to count - 1 of a device hold live requests. `lengths`: positions 0 to length - 1 of a request slot's cache are live.
All inputs are finite; a program needn't handle non-finite values.
Results may differ from the reference program's by a relative error of at most 0.006.
Values may be sent and summed in bfloat16 or wider, within the bound.
A program may use at most 64 MiB of HBM per device.

```python
import jax
import jax.numpy as jnp
from jax import lax

MODEL = 7168
HEADS = 128
LATENT = 512
HEAD_DIM = 128
SLOTS = 2
CONTEXT = 1024
CACHE_DIM = 576
REQUESTS = 1024


def first_latents(key):
    return jnp.clip(jax.random.normal(jax.random.fold_in(key, 101), (REQUESTS, CACHE_DIM), jnp.float32), -4.0, 4.0)


def draw_latent_cache(key, part):
    leading = first_latents(key)
    key = jax.random.fold_in(key, 7)
    latents = jnp.clip(jax.random.normal(key, (REQUESTS, CONTEXT, CACHE_DIM), jnp.float32), -4.0, 4.0)
    latents = latents.at[:, 0, :].set(leading)
    return latents.astype(jnp.bfloat16)


def draw_queries(key, part):
    key = jax.random.fold_in(key, 13)
    spread = 1.5 * (192.0 / CACHE_DIM) ** 0.5
    drawn = spread * jnp.clip(jax.random.normal(key, (REQUESTS, HEADS, CACHE_DIM), jnp.float32), -6.0, 6.0)
    return drawn.astype(jnp.bfloat16)


def draw_lengths(key, part):
    key = jax.random.fold_in(key, 5)
    left_key, right_key, spot_key = jax.random.split(key, 3)
    lengths = jnp.minimum(jax.random.randint(left_key, (REQUESTS,), 2, CONTEXT + 1), jax.random.randint(right_key, (REQUESTS,), 2, CONTEXT + 1))
    longest = jax.random.randint(spot_key, (), 0, REQUESTS // SLOTS) * SLOTS
    return lengths.at[longest].set(CONTEXT).astype(jnp.int32)


def draw_counts(key, part):
    key = jax.random.fold_in(key, 3)
    left_key, spot_key = jax.random.split(key, 2)
    counts = jax.random.randint(left_key, (REQUESTS // SLOTS,), 1, SLOTS + 1)
    fullest = jax.random.randint(spot_key, (), 0, REQUESTS // SLOTS)
    return counts.at[fullest].set(SLOTS).astype(jnp.int32)


def steps_of(key, dims, pieces, smallest, high):
    loudness = 1.0
    for dim, blocks in pieces:
        draws = jax.random.uniform(jax.random.fold_in(jax.random.fold_in(key, 6), dim), (blocks,), jnp.float32, smallest / len(pieces), high / len(pieces))
        loudness = loudness * jnp.repeat(jnp.exp(draws), dims[dim] // blocks).reshape((-1,) + (1,) * (len(dims) - 1 - dim))
    return loudness


def bell_draw(key, extent, scale, reach, pieces=(), kind=jnp.bfloat16):
    values = jax.random.normal(key, extent, jnp.float32) * scale
    if len(pieces) > 0:
        values = steps_of(key, extent, pieces, -0.22, 0.18) * values
    return jnp.clip(values, min=-reach, max=reach).astype(kind)


def setup_inputs(seed: int = 0) -> dict:
    arg_keys = jax.random.split(jax.random.key(seed), 8)
    return {
        "queries": draw_queries(jax.random.fold_in(arg_keys[7], 71), 0),
        "latent_cache": draw_latent_cache(jax.random.fold_in(arg_keys[7], 71), 0),
        "lengths": draw_lengths(jax.random.fold_in(arg_keys[7], 71), 0),
        "counts": draw_counts(jax.random.fold_in(arg_keys[7], 71), 0),
        "value_up": bell_draw(arg_keys[4], (HEADS, LATENT, HEAD_DIM), (6.0 / LATENT ** 0.5), 4.0, ((0, 32),)),
        "out_proj": bell_draw(arg_keys[5], (HEADS * HEAD_DIM, MODEL), (2.0 / (HEADS * HEAD_DIM) ** 0.5), 0.25, ((0, 32), (1, 16))),
        "residual": bell_draw(arg_keys[6], (REQUESTS, MODEL), 1.0, 6.0, ((0, 32), (1, 16))),
    }


softmax_scale = 192.0 ** -0.5


def attend_rows(operands):
    query_rows, cache_rows, length_rows, live_rows = operands
    scores = jnp.einsum('rhc,rjc->rhj', query_rows.astype(jnp.float32), cache_rows.astype(jnp.float32)) * softmax_scale
    position = jnp.arange(CONTEXT, dtype=jnp.int32)
    in_range = position[None, None, :] < length_rows[:, None, None]
    scores = jnp.where(in_range, scores, -jnp.inf)
    row_max = jnp.max(scores, axis=-1, keepdims=True)
    exponent = jnp.exp(scores - row_max)
    weights = (exponent / jnp.sum(exponent, axis=-1, keepdims=True)).astype(jnp.bfloat16)
    attended = jnp.einsum('rhj,rjc->rhc', weights.astype(jnp.float32), cache_rows[:, :, :LATENT].astype(jnp.float32))
    attended = jnp.where(live_rows[:, None, None], attended, 0.0)
    return attended.astype(jnp.bfloat16)


def reference(queries, latent_cache, lengths, counts, value_up, out_proj, residual):
    row_ids = jnp.arange(REQUESTS, dtype=jnp.int32)
    live = (row_ids % SLOTS) < counts[row_ids // SLOTS]
    groups = REQUESTS // SLOTS
    attended = lax.map(attend_rows, (queries.reshape(groups, SLOTS, HEADS, CACHE_DIM),
                                     latent_cache.reshape(groups, SLOTS, CONTEXT, CACHE_DIM),
                                     lengths.reshape(groups, SLOTS),
                                     live.reshape(groups, SLOTS)))
    attended = attended.reshape(REQUESTS, HEADS, LATENT)
    values = jnp.einsum('rhc,hce->rhe', attended.astype(jnp.float32), value_up.astype(jnp.float32)).astype(jnp.bfloat16)
    head_total = jnp.dot(values.reshape(REQUESTS, HEADS * HEAD_DIM), out_proj, preferred_element_type=jnp.float32)
    return (residual.astype(jnp.float32) + head_total).astype(jnp.bfloat16)
```

```python
import functools
import math

import jax
import jax.numpy as jnp
from jax import lax
from jax.experimental import pallas as pl
from jax.experimental.pallas import tpu as pltpu
from jax.sharding import PartitionSpec as P

MESH = pl.DeviceIdType.MESH
LANES = 128
NX = 4
SCALE = 192.0 ** (-0.5)
F32 = jnp.float32
BF16 = jnp.bfloat16


def one_hot(rows, cols, column_of_row):
    row = lax.broadcasted_iota(jnp.int32, (rows, cols), 0)
    col = lax.broadcasted_iota(jnp.int32, (rows, cols), 1)
    return (col == column_of_row(row)).astype(F32).astype(BF16)


def dot(a, b):
    return jnp.dot(a, b, preferred_element_type=F32)


def kernel(
    nd, nt, len_ref, cnt_ref, q_hbm, c_hbm, w_hbm, o_hbm, r_hbm, out_ref,
    qv, cv, wv, ov, rv, snd, rcv, gath, part, xsnd, xrcv, ysnd, yrcv, acc,
    load_sem, a_send, a_recv, g_send, g_recv, c_recv, x_send, x_recv, y_send, y_recv,
):
    nz = nd // 2
    d, t = lax.axis_index("dp"), lax.axis_index("tp")
    z, c = d // 2, d % 2
    y, x = t // NX, t % NX
    up = (2 * ((z + 1) % nz) + c, t)
    down = (2 * ((z + nz - 1) % nz) + c, t)
    other = (2 * z + 1 - c, t)
    slots, heads, _ = q_hbm.shape
    local, latent, width = w_hbm.shape
    pieces = latent // LANES
    block = local * pieces

    def load(i, src, dst):
        return pltpu.make_async_copy(src, dst, load_sem.at[i])

    loads = []
    for s in range(slots):
        loads.append((load(2 * s, q_hbm.at[s], qv.at[s]), load(2 * s + 1, c_hbm.at[s], cv.at[s])))
    late = [load(4, w_hbm, wv), load(5, o_hbm, ov), load(6, r_hbm, rv)]
    for pair in loads:
        for copy in pair:
            copy.start()
    for copy in late:
        copy.start()

    barrier = pltpu.get_barrier_semaphore()

    def greet(j, carry):
        pl.semaphore_signal(barrier, inc=1, device_id=(d, (t + j) % nt), device_id_type=MESH)
        return carry

    lax.fori_loop(1, nt, greet, 0)
    for device in (up, down, other):
        pl.semaphore_signal(barrier, inc=1, device_id=device, device_id_type=MESH)

    to_owner = one_hot(
        heads * pieces, heads * pieces,
        lambda r: ((r // local) % pieces) * heads + (r // block) * local + r % local,
    )
    for s in range(slots):
        for copy in loads[s]:
            copy.wait()
        scores = lax.dot_general(qv[s], cv[s], (((1,), (1,)), ((), ())), preferred_element_type=F32)
        position = lax.broadcasted_iota(jnp.int32, scores.shape, 1)
        scores = jnp.where(position < len_ref[s], scores, -jnp.inf)
        top = jnp.max(scores, axis=1, keepdims=True)
        weight = jnp.exp2((scores - top) * (SCALE * math.log2(math.e)))
        weight = (weight * (1.0 / jnp.sum(weight, axis=1, keepdims=True))).astype(BF16)
        attended = dot(weight, cv[s, :, :latent])
        attended = jnp.where(cnt_ref[0] > s, attended, 0.0).astype(BF16)
        stacked = jnp.concatenate([attended[:, k * LANES:(k + 1) * LANES] for k in range(pieces)], axis=0)
        snd[s] = dot(to_owner, stacked).astype(BF16).reshape(nt, block, LANES)
        if s == 0:
            pl.semaphore_wait(barrier, nt - 1 + 3)

        def scatter(j, carry, s=s):
            to = (t + j) % nt
            pltpu.make_async_remote_copy(
                src_ref=snd.at[s, to], dst_ref=rcv.at[s, t], send_sem=a_send.at[s], recv_sem=a_recv.at[s],
                device_id=(d, to), device_id_type=MESH,
            ).start()
            return carry

        lax.fori_loop(1, nt, scatter, 0)
        rcv[s, t] = snd[s, t]

    for copy in late:
        copy.wait()

    by_head = one_hot(nt * block, nt * block, lambda r: (r % nt) * block + r // nt)
    arrived = []
    for s in range(slots):
        every = rcv.at[s, pl.ds(0, nt - 1)]
        pltpu.make_async_copy(every, every, a_recv.at[s]).wait()
        arrived.append(dot(by_head, rcv[s].reshape(nt * block, LANES)).astype(BF16))
    values = []
    for h in range(local):
        rows = []
        for s in range(slots):
            starts = [(k * local + h) * nt for k in range(pieces)]
            rows.append(jnp.concatenate([arrived[s][a:a + nt] for a in starts], axis=1))
        values.append(dot(jnp.concatenate(rows, axis=0), wv[h]).astype(BF16))
    mine = slots * nt
    in_order = one_hot(mine, mine, lambda r: (r % slots) * nt + r // slots)
    gath[d] = dot(in_order, jnp.concatenate(values, axis=1)).astype(BF16)

    half = mine // 2

    def send(ref, sem, device):
        pltpu.make_async_remote_copy(
            src_ref=ref, dst_ref=ref, send_sem=g_send, recv_sem=sem, device_id=device, device_id_type=MESH
        ).start()

    def arrival(ref, sem):
        pltpu.make_async_copy(ref, ref, sem).wait()

    last = nz // 2 - 1
    for p in range(2):
        for way in range(2):
            send(gath.at[d, pl.ds(p * half, half)], g_recv.at[way, 0, p], (up, down)[way])
    send(gath.at[d], c_recv.at[0, nz // 2, 0], other)

    def origin(way, step):
        return (z + nz - step - 1) % nz if way == 0 else (z + step + 1) % nz

    rows_out = out_ref.shape[0]

    def project(i, chip):
        rows = gath[pl.ds(2 * chip, 2)].reshape(2 * mine, local * width)
        product = dot(rows, ov[...]).reshape(NX, rows_out, out_ref.shape[1])
        part[i] = product
        xsnd[i] = product.astype(BF16)
        for j in range(1, NX):
            to = (x + j) % NX
            pltpu.make_async_remote_copy(
                src_ref=xsnd.at[i, to], dst_ref=xrcv.at[i, j - 1], send_sem=x_send, recv_sem=x_recv.at[i],
                device_id=(d, y * NX + to), device_id_type=MESH,
            ).start()

    def reduce_x(i, chip):
        arrival(xrcv.at[i], x_recv.at[i])
        total = part[i, x]
        for j in range(NX - 1):
            total += xrcv[i, j].astype(F32)
        ysnd[i] = total.astype(BF16)

        @pl.when(chip != y)
        def _():
            pltpu.make_async_remote_copy(
                src_ref=ysnd.at[i], dst_ref=yrcv.at[y], send_sem=y_send, recv_sem=y_recv,
                device_id=(d, chip * NX + x), device_id_type=MESH,
            ).start()

        @pl.when(chip == y)
        def _():
            acc[...] = total
            yrcv[y] = jnp.zeros_like(ysnd[i])

    arrival(gath.at[2 * z + 1 - c], c_recv.at[0, nz // 2, 0])
    project(0, z)
    done = [(0, z)]
    for step in range(nz // 2):
        for p in range(2):
            for way in range(2):
                if step == last and p != way:
                    continue
                ref = gath.at[2 * origin(way, step) + c, pl.ds(p * half, half)]
                arrival(ref, g_recv.at[way, step, p])
                if step < last - 1 or (step == last - 1 and p == way):
                    send(ref, g_recv.at[way, step + 1, p], (up, down)[way])
                send(ref, c_recv.at[way, step, p], other)
        for way in range(2):
            for p in range(2):
                if step == last and p != way:
                    continue
                ref = gath.at[2 * origin(way, step) + 1 - c, pl.ds(p * half, half)]
                arrival(ref, c_recv.at[way, step, p])
        ready = []
        for way in range(2 if step < last else 1):
            i = 2 * step + 1 + way
            project(i, origin(way, step))
            ready.append((i, origin(way, step)))
        for i, chip in done:
            reduce_x(i, chip)
        done = ready
    for i, chip in done:
        reduce_x(i, chip)

    every = yrcv.at[pl.ds(0, nz - 1)]
    pltpu.make_async_copy(every, every, y_recv).wait()
    total = rv[...].astype(F32) + acc[...]
    for i in range(nz):
        total += yrcv[i].astype(F32)
    out_ref[...] = total.astype(BF16)

    for s in range(slots):
        every = snd.at[s, pl.ds(0, nt - 1)]
        pltpu.make_async_copy(every, every, a_send.at[s]).wait()
    every = gath.at[pl.ds(0, nd - 1)]
    pltpu.make_async_copy(every, every, g_send).wait()
    every = xsnd.at[:, pl.ds(0, NX - 1)]
    pltpu.make_async_copy(every, every, x_send).wait()
    every = ysnd.at[pl.ds(0, nz - 1)]
    pltpu.make_async_copy(every, every, y_send).wait()


def body(queries, latent_cache, lengths, counts, value_up, out_proj, residual, nd, nt):
    slots, heads, _ = queries.shape
    local, latent, width = value_up.shape
    nz = nd // 2
    rows, columns = residual.shape
    block = local * latent // LANES
    any_spec = pl.BlockSpec(memory_space=pl.ANY)
    smem_spec = pl.BlockSpec(memory_space=pltpu.SMEM)
    vmem, dma = pltpu.VMEM, pltpu.SemaphoreType.DMA
    return pl.pallas_call(
        functools.partial(kernel, nd, nt),
        out_shape=jax.ShapeDtypeStruct((rows, columns), BF16),
        in_specs=[smem_spec, smem_spec] + [any_spec] * 5,
        out_specs=pl.BlockSpec(memory_space=pltpu.VMEM),
        scratch_shapes=[
            vmem(queries.shape, BF16),
            vmem(latent_cache.shape, BF16),
            vmem(value_up.shape, BF16),
            vmem(out_proj.shape, BF16),
            vmem(residual.shape, BF16),
            vmem((slots, nt, block, LANES), BF16),
            vmem((slots, nt, block, LANES), BF16),
            vmem((nd, slots * nt, local * width), BF16),
            vmem((nz, NX, rows, columns), F32),
            vmem((nz, NX, rows, columns), BF16),
            vmem((nz, NX - 1, rows, columns), BF16),
            vmem((nz, rows, columns), BF16),
            vmem((nz, rows, columns), BF16),
            vmem((rows, columns), F32),
            dma((7,)), dma((slots,)), dma((slots,)), dma, dma((2, nz // 2, 2)), dma((2, nz // 2 + 1, 2)),
            dma, dma((nz,)), dma, dma,
        ],
        compiler_params=pltpu.CompilerParams(
            collective_id=0, has_side_effects=True, vmem_limit_bytes=48 * 1024 * 1024
        ),
        name="decode_attention",
    )(lengths, counts, queries, latent_cache, value_up, out_proj, residual)


def solution(mesh):
    in_specs = (
        P(("dp", "tp"), None, None),
        P(("dp", "tp"), None, None),
        P(("dp", "tp")),
        P(("dp", "tp")),
        P("tp", None, None),
        P("tp", "dp"),
        P("tp", "dp"),
    )
    step = functools.partial(body, nd=mesh.shape["dp"], nt=mesh.shape["tp"])
    return jax.shard_map(step, mesh=mesh, in_specs=in_specs, out_specs=P("tp", "dp"), check_vma=False)
```

```python
import functools
import math

import jax
import jax.numpy as jnp
from jax import lax
from jax.experimental import pallas as pl
from jax.experimental.pallas import tpu as pltpu
from jax.sharding import PartitionSpec as P

MESH = pl.DeviceIdType.MESH
LANES = 128
NX = 4
VMEM_LIMIT = 60 * 1024 * 1024
SCALE = 192.0 ** (-0.5)
F32 = jnp.float32
BF16 = jnp.bfloat16


def one_hot(rows, cols, column_of_row):
    row = lax.broadcasted_iota(jnp.int32, (rows, cols), 0)
    col = lax.broadcasted_iota(jnp.int32, (rows, cols), 1)
    return (col == column_of_row(row)).astype(F32).astype(BF16)


def dot(a, b):
    return jnp.dot(a, b, preferred_element_type=F32)


def kernel(
    nd, nt, len_ref, cnt_ref, q_hbm, c_hbm, w_hbm, o_hbm, r_hbm, out_ref,
    qv, cv, wv, ov, rv, owner_map, head_map, snd, rcv, vals, gath, ysnd, yrcv, acc,
    load_sem, a_send, a_recv, o_send, o_recv, g_send, g_recv, near_send, near_recv, r_send, c_send, c_recv, y_send, y_recv,
):
    nz = nd // 2
    d, t = lax.axis_index("dp"), lax.axis_index("tp")
    z, c = d // 2, d % 2
    y, x = t // NX, t % NX
    other = (2 * z + 1 - c, t)
    alone = x == 3 * c
    slots = q_hbm.shape[0]
    heads = q_hbm.shape[2]
    local, latent, width = w_hbm.shape
    pieces = latent // LANES
    block = local * pieces
    rows_out, columns = out_ref.shape
    part = rows_out // slots
    direct = (2, nz - 2, 1, nz - 1, 0)

    def load(i, src, dst):
        return pltpu.make_async_copy(src, dst, load_sem.at[i])

    loads = [(load(2 * s, q_hbm.at[s], qv.at[s]), load(2 * s + 1, c_hbm.at[s], cv.at[s])) for s in range(slots)]
    late = [load(4, w_hbm, wv), load(5, o_hbm, ov.at[x]), load(6, r_hbm, rv)]
    for pair in loads:
        for copy in pair:
            copy.start()
    for copy in late:
        copy.start()

    barrier = pltpu.get_barrier_semaphore()

    def greet(device):
        pl.semaphore_signal(barrier, inc=1, device_id=device, device_id_type=MESH)

    def greet_peer(j, carry):
        greet((d, (t + j) % nt))
        return carry

    lax.fori_loop(1, nt, greet_peer, 0)
    greet(other)
    for dz in direct[:-1]:
        greet((2 * ((z + dz) % nz) + c, t))
    for dz in direct:
        for f in range(2):
            source = (2 * ((z + nz - dz) % nz) + x // 2, y * NX + c + 2 * f)
            if dz == 0:
                @pl.when(jnp.logical_not(jnp.logical_and(alone, f == c)))
                def _():
                    greet(source)
            else:
                greet(source)

    owner_map[...] = one_hot(
        heads * pieces, heads * pieces,
        lambda r: ((r // local) % pieces) * heads + (r // block) * local + r % local,
    )
    head_map[...] = one_hot(nt * block, nt * block, lambda r: (r % nt) * block + r // nt)
    for s in range(slots):
        for copy in loads[s]:
            copy.wait()
        scores = lax.dot_general(qv[s], cv[s], (((0,), (0,)), ((), ())), preferred_element_type=F32)
        position = lax.broadcasted_iota(jnp.int32, scores.shape, 1)
        scores = jnp.where(position < len_ref[s], scores, -jnp.inf)
        top = jnp.max(scores, axis=1, keepdims=True)
        weight = jnp.exp2((scores - top) * (SCALE * math.log2(math.e)))
        weight = (weight * (1.0 / jnp.sum(weight, axis=1, keepdims=True))).astype(BF16)
        attended = lax.dot_general(weight, cv[s, :latent], (((1,), (1,)), ((), ())), preferred_element_type=F32)
        attended = jnp.where(cnt_ref[0] > s, attended, 0.0).astype(BF16)
        stacked = jnp.concatenate([attended[:, k * LANES:(k + 1) * LANES] for k in range(pieces)], axis=0)
        snd[s] = dot(owner_map[...], stacked).astype(BF16).reshape(nt, block, LANES)
        if s == 0:
            pl.semaphore_wait(barrier, nt + 3 * len(direct) - 1 - alone.astype(jnp.int32))

        def scatter(j, carry, s=s):
            to = (t + j) % nt
            pltpu.make_async_remote_copy(
                src_ref=snd.at[s, to], dst_ref=rcv.at[s, t], send_sem=a_send.at[s], recv_sem=a_recv.at[s],
                device_id=(d, to), device_id_type=MESH,
            ).start()
            return carry

        lax.fori_loop(1, nt, scatter, 0)
        rcv[s, t] = snd[s, t]

    for copy in late:
        copy.wait()

    low, high = pl.ds(0, columns // 2), pl.ds(columns // 2, columns // 2)
    left, right = (d, y * NX + (x + NX - 1) % NX), (d, y * NX + (x + 1) % NX)

    def turn(owner, rows, sem, device):
        ref = ov.at[owner, rows]
        pltpu.make_async_remote_copy(
            src_ref=ref, dst_ref=ref, send_sem=o_send, recv_sem=o_recv.at[sem], device_id=device, device_id_type=MESH
        ).start()

    turn(x, low, 0, left)
    turn(x, high, 1, right)
    turn(x, high, 2, left)
    turn(x, low, 3, right)
    residual = dot(one_hot(rows_out, rows_out, lambda r: (r % part) * slots + r // part), rv[...])

    def wait(ref, sem):
        pltpu.make_async_copy(ref, ref, sem).wait()

    wait(ov.at[(x + 1) % NX, low], o_recv.at[0])
    turn((x + 1) % NX, low, 4, left)
    wait(ov.at[(x + NX - 1) % NX, high], o_recv.at[1])
    turn((x + NX - 1) % NX, high, 5, right)

    for s in range(slots):
        wait(rcv.at[s, pl.ds(0, nt - 1)], a_recv.at[s])
        arrived = dot(head_map[...], rcv[s].reshape(nt * block, LANES)).astype(BF16)
        values = []
        for h in range(local):
            starts = [(k * local + h) * nt for k in range(pieces)]
            rows = jnp.concatenate([arrived[a:a + nt] for a in starts], axis=1)
            values.append(dot(rows, wv[h]).astype(BF16))
        vals[s] = jnp.concatenate(values, axis=1).reshape(2, part, local * width)
        for dz in direct:
            for e in range(2):
                copy = pltpu.make_async_remote_copy(
                    src_ref=vals.at[s, e], dst_ref=gath.at[z, x % 2, s, x // 2],
                    send_sem=g_send.at[dz] if dz else near_send.at[e],
                    recv_sem=g_recv.at[dz, s] if dz else near_recv.at[x // 2],
                    device_id=(2 * ((z + dz) % nz) + x % 2, y * NX + 2 * c + e), device_id_type=MESH,
                )
                if dz:
                    copy.start()
                else:
                    @pl.when(jnp.logical_not(jnp.logical_and(alone, x % 2 == e)))
                    def _():
                        copy.start()

        @pl.when(alone)
        def _():
            gath[z, c, s, x // 2] = vals[s, x % 2]

    def hand(ref, sem):
        pltpu.make_async_remote_copy(
            src_ref=ref, dst_ref=ref, send_sem=c_send, recv_sem=sem, device_id=other, device_id_type=MESH
        ).start()

    def pass_on(dz, s, steps):
        ref = gath.at[(z + nz - dz) % nz, c, s]
        wait(ref, g_recv.at[dz, s])
        for step in steps:
            pltpu.make_async_remote_copy(
                src_ref=ref, dst_ref=ref, send_sem=r_send, recv_sem=g_recv.at[(dz + step) % nz, s],
                device_id=(2 * ((z + nz + step) % nz) + c, t), device_id_type=MESH,
            ).start()
        hand(ref, c_recv.at[dz, s])

    far = nz // 2
    for s in range(slots):
        pass_on(2, s, (1, 2) if s == 0 else (1,))
        pass_on(nz - 2, s, (-1, -2) if s == 1 else (-1,))
    for dz in (1, nz - 1):
        for s in range(slots):
            pass_on(dz, s, ())
    for f in range(2):
        @pl.when(jnp.logical_not(jnp.logical_and(alone, f == c)))
        def _():
            wait(gath.at[z, c, :, f], near_recv.at[f])
    for s in range(slots):
        hand(gath.at[z, c, s], c_recv.at[0, s])

    def project(batch):
        origins = [(z + nz - dz) % nz for dz in batch]
        for dz, origin in zip(batch, origins):
            for s in range(slots):
                wait(gath.at[origin, 1 - c, s], c_recv.at[dz, s])
        product = None
        for source in range(NX):
            rows = [gath[o, source % 2, s, source // 2] for o in origins for s in range(slots)]
            term = lax.dot_general(
                jnp.concatenate(rows, axis=0), ov[source], (((1,), (1,)), ((), ())), preferred_element_type=F32
            )
            product = term if product is None else product + term
        for i, (dz, origin) in enumerate(zip(batch, origins)):
            piece = product[i * rows_out:(i + 1) * rows_out]
            ysnd[dz] = piece.astype(BF16)

            @pl.when(origin != y)
            def _():
                pltpu.make_async_remote_copy(
                    src_ref=ysnd.at[dz], dst_ref=yrcv.at[y], send_sem=y_send, recv_sem=y_recv,
                    device_id=(d, origin * NX + x), device_id_type=MESH,
                ).start()

            @pl.when(origin == y)
            def _():
                acc[...] = piece
                yrcv[y] = jnp.zeros_like(ysnd[dz])

    for owner, rows, sem in ((x + 1, high, 2), (x + NX - 1, low, 3), (x + 2, low, 4), (x + 2, high, 5)):
        wait(ov.at[owner % NX, rows], o_recv.at[sem])
    project((0, 1, nz - 1, 2, nz - 2))
    for dz in (3, nz - 3, far):
        for s in range(slots):
            pass_on(dz, s, ())
    project((3, nz - 3, far))

    wait(yrcv.at[pl.ds(0, nz - 1)], y_recv)
    total = residual + acc[...]
    for i in range(nz):
        total += yrcv[i].astype(F32)
    back = one_hot(rows_out, rows_out, lambda r: (r % slots) * part + r // slots)
    out_ref[...] = dot(back, total.astype(BF16)).astype(BF16)

    for s in range(slots):
        wait(snd.at[s, pl.ds(0, nt - 1)], a_send.at[s])
    wait(ov.at[pl.ds(0, NX - 1)], o_send)
    for dz in direct[:-1]:
        wait(vals, g_send.at[dz])
    for e in range(2):
        @pl.when(jnp.logical_not(jnp.logical_and(alone, x % 2 == e)))
        def _():
            wait(gath.at[0, 0, 0], near_send.at[e])
    wait(gath.at[pl.ds(0, 3), 0], r_send)
    wait(gath.at[:, 0], c_send)
    wait(ysnd.at[pl.ds(0, nz - 1)], y_send)


def body(queries, latent_cache, lengths, counts, value_up, out_proj, residual, nd, nt):
    queries, latent_cache, out_proj = queries.swapaxes(1, 2), latent_cache.swapaxes(1, 2), out_proj.T
    slots, _, heads = queries.shape
    local, latent, width = value_up.shape
    nz = nd // 2
    rows, columns = residual.shape
    part = rows // slots
    block = local * latent // LANES
    any_spec = pl.BlockSpec(memory_space=pl.ANY)
    smem_spec = pl.BlockSpec(memory_space=pltpu.SMEM)
    vmem, dma = pltpu.VMEM, pltpu.SemaphoreType.DMA
    return pl.pallas_call(
        functools.partial(kernel, nd, nt),
        out_shape=jax.ShapeDtypeStruct((rows, columns), BF16),
        in_specs=[smem_spec, smem_spec] + [any_spec] * 5,
        out_specs=pl.BlockSpec(memory_space=pltpu.VMEM),
        scratch_shapes=[
            vmem(queries.shape, BF16),
            vmem(latent_cache.shape, BF16),
            vmem(value_up.shape, BF16),
            vmem((NX,) + out_proj.shape, BF16),
            vmem(residual.shape, BF16),
            vmem((nt * block, nt * block), BF16),
            vmem((nt * block, nt * block), BF16),
            vmem((slots, nt, block, LANES), BF16),
            vmem((slots, nt, block, LANES), BF16),
            vmem((slots, 2, part, local * width), BF16),
            vmem((nz, 2, slots, 2, part, local * width), BF16),
            vmem((nz, rows, columns), BF16),
            vmem((nz, rows, columns), BF16),
            vmem((rows, columns), F32),
            dma((7,)), dma((slots,)), dma((slots,)), dma, dma((6,)), dma((nz,)), dma((nz, slots)), dma((2,)), dma((2,)),
            dma, dma, dma((nz, slots)), dma, dma,
        ],
        compiler_params=pltpu.CompilerParams(
            collective_id=0, has_side_effects=True, vmem_limit_bytes=VMEM_LIMIT
        ),
        name="decode_attention",
    )(lengths, counts, queries, latent_cache, value_up, out_proj, residual)


def solution(mesh):
    in_specs = (
        P(("dp", "tp"), None, None),
        P(("dp", "tp"), None, None),
        P(("dp", "tp")),
        P(("dp", "tp")),
        P("tp", None, None),
        P("tp", "dp"),
        P("tp", "dp"),
    )
    step = functools.partial(body, nd=mesh.shape["dp"], nt=mesh.shape["tp"])
    return jax.shard_map(step, mesh=mesh, in_specs=in_specs, out_specs=P("tp", "dp"), check_vma=False)
```

```python
import functools
import math

import jax
import jax.numpy as jnp
from jax import lax
from jax.experimental import pallas as pl
from jax.experimental.pallas import tpu as pltpu
from jax.sharding import PartitionSpec as P

MESH = pl.DeviceIdType.MESH
LANES = 128
NX = 4
VMEM_LIMIT = 55168 * 1024
SCALE = 192.0 ** (-0.5)
F32 = jnp.float32
BF16 = jnp.bfloat16


def one_hot(rows, cols, column_of_row):
    row = lax.broadcasted_iota(jnp.int32, (rows, cols), 0)
    col = lax.broadcasted_iota(jnp.int32, (rows, cols), 1)
    return (col == column_of_row(row)).astype(F32).astype(BF16)


def outward(i, n):
    return n // 2 + jnp.where(i % 2 == 1, -((i + 1) // 2), i // 2)


def dot(a, b):
    return jnp.dot(a, b, preferred_element_type=F32)


def kernel(
    nd, nt, len_hbm, cnt_hbm, q_hbm, c_hbm, w_hbm, o_hbm, r_hbm, out_ref,
    len_ref, cnt_ref, qv, cv, wv, ov, rv, owner_map, head_map, snd, rcv, vals, gath, ysnd, yrcv, acc,
    load_sem, a_send, a_recv, o_send, o_recv, g_send, g_recv, near_send, near_recv, r_send, c_send, c_recv, y_send, y_recv,
):
    nz = nd // 2
    d, t = lax.axis_index("dp"), lax.axis_index("tp")
    z, c = d // 2, d % 2
    y, x = t // NX, t % NX
    other = (2 * z + 1 - c, t)
    alone = x == 3 * c
    slots = q_hbm.shape[0]
    heads = q_hbm.shape[2]
    local, latent, width = w_hbm.shape
    pieces = latent // LANES
    block = local * pieces
    rows_out, columns = out_ref.shape
    part = rows_out // slots
    direct = (2, nz - 2, 1, nz - 1, 0)

    def load(i, src, dst):
        return pltpu.make_async_copy(src, dst, load_sem.at[i])

    loads = [(load(2 * s, q_hbm.at[s], qv.at[s]), load(2 * s + 1, c_hbm.at[s], cv.at[s])) for s in range(slots)]
    late = [load(4, w_hbm, wv), load(5, o_hbm, ov.at[x]), load(6, r_hbm, rv)]
    loads[0] += (load(7, len_hbm, len_ref), load(8, cnt_hbm, cnt_ref))
    for copy in loads[0]:
        copy.start()

    barrier = pltpu.get_barrier_semaphore()

    def greet(device):
        pl.semaphore_signal(barrier, inc=1, device_id=device, device_id_type=MESH)

    def greet_peer(j, carry):
        greet((d, (t + j) % nt))
        return carry

    lax.fori_loop(1, nt, greet_peer, 0)
    greet(other)
    for dz in direct[:-1]:
        greet((2 * ((z + dz) % nz) + c, t))
    for dz in direct:
        for f in range(2):
            source = (2 * ((z + nz - dz) % nz) + x // 2, y * NX + c + 2 * f)
            if dz == 0:
                @pl.when(jnp.logical_not(jnp.logical_and(alone, f == c)))
                def _():
                    greet(source)
            else:
                greet(source)

    owner_map[...] = one_hot(
        heads * pieces, heads * pieces,
        lambda r: ((r // local) % pieces) * heads + (r // block) * local + r % local,
    )
    for s in range(slots):
        for copy in loads[s]:
            copy.wait()
        for copy in loads[s + 1] if s + 1 < slots else late:
            copy.start()
        scores = lax.dot_general(qv[s], cv[s], (((0,), (0,)), ((), ())), preferred_element_type=F32)
        position = lax.broadcasted_iota(jnp.int32, scores.shape, 1)
        scores = jnp.where(position < len_ref[s], scores, -jnp.inf)
        top = jnp.max(scores, axis=1, keepdims=True)
        weight = jnp.exp2((scores - top) * (SCALE * math.log2(math.e)))
        weight = (weight * (1.0 / jnp.sum(weight, axis=1, keepdims=True))).astype(BF16)
        attended = lax.dot_general(weight, cv[s, :latent], (((1,), (1,)), ((), ())), preferred_element_type=F32)
        attended = jnp.where(cnt_ref[0] > s, attended, 0.0).astype(BF16)
        stacked = jnp.concatenate([attended[:, k * LANES:(k + 1) * LANES] for k in range(pieces)], axis=0)
        snd[:, s] = dot(owner_map[...], stacked).astype(BF16).reshape(nt, block, LANES)
    pl.semaphore_wait(barrier, nt + 3 * len(direct) - 1 - alone.astype(jnp.int32))

    for copy in late:
        copy.wait()

    low, high = pl.ds(0, columns // 2), pl.ds(columns // 2, columns // 2)
    left, right = (d, y * NX + (x + NX - 1) % NX), (d, y * NX + (x + 1) % NX)

    def turn(*moves, starts=range(0, columns // 2, 32)):
        for start in starts:
            for owner, rows, sem, device in moves:
                ref = ov.at[owner, pl.ds(rows.start + start, 32)]
                pltpu.make_async_remote_copy(
                    src_ref=ref, dst_ref=ref, send_sem=o_send, recv_sem=o_recv.at[sem],
                    device_id=device, device_id_type=MESH,
                ).start()

    def scatter(i, carry):
        to = (y + outward(i // NX, nt // NX)) % (nt // NX) * NX + (x + outward(i % NX, NX)) % NX
        pltpu.make_async_remote_copy(
            src_ref=snd.at[to], dst_ref=rcv.at[t], send_sem=a_send, recv_sem=a_recv,
            device_id=(d, to), device_id_type=MESH,
        ).start()
        return carry

    lax.fori_loop(0, 16, scatter, 0)
    for n, start in enumerate(range(0, columns // 2, 32)):
        lax.fori_loop(16 + 2 * n, 16 + 2 * n + 2, scatter, 0)
        turn((x, low, 0, left), (x, high, 1, right), starts=(start,))
    lax.fori_loop(16 + columns // 32, nt - 1, scatter, 0)
    rcv[t] = snd[t]

    head_map[...] = one_hot(nt * block, nt * block, lambda r: (r % nt) * block + r // nt)
    turn((x, high, 2, left), (x, low, 3, right))
    residual = dot(one_hot(rows_out, rows_out, lambda r: (r % part) * slots + r // part), rv[...])

    def wait(ref, sem):
        pltpu.make_async_copy(ref, ref, sem).wait()

    wait(rcv.at[pl.ds(0, nt - 1)], a_recv)
    arrived = jnp.concatenate([rcv[:, s].reshape(nt * block, LANES) for s in range(slots)], axis=1)
    arrived = dot(head_map[...], arrived).astype(BF16)
    values = []
    for h in range(local):
        rows = []
        for s in range(slots):
            starts = [(k * local + h) * nt for k in range(pieces)]
            rows.append(jnp.concatenate([arrived[a:a + nt, s * LANES:(s + 1) * LANES] for a in starts], axis=1))
        values.append(dot(jnp.concatenate(rows, axis=0), wv[h]).astype(BF16))
    vals[...] = jnp.concatenate(values, axis=1).reshape(slots, 2, part, local * width)

    def spread(dz, s):
        for e in range(2):
            copy = pltpu.make_async_remote_copy(
                src_ref=vals.at[s, e], dst_ref=gath.at[z, x % 2, s, x // 2],
                send_sem=g_send.at[dz] if dz else near_send.at[e],
                recv_sem=g_recv.at[dz, s] if dz else near_recv.at[x // 2],
                device_id=(2 * ((z + dz) % nz) + x % 2, y * NX + 2 * c + e), device_id_type=MESH,
            )
            if dz:
                copy.start()
            else:
                @pl.when(jnp.logical_not(jnp.logical_and(alone, x % 2 == e)))
                def _():
                    copy.start()

    for dz, s in ((2, 0), (nz - 2, 1), (2, 1), (nz - 2, 0)):
        spread(dz, s)
    for dz in (0, 1, nz - 1):
        for s in range(slots):
            spread(dz, s)

    for s in range(slots):
        @pl.when(alone)
        def _():
            gath[z, c, s, x // 2] = vals[s, x % 2]

    def hand(ref, sem):
        pltpu.make_async_remote_copy(
            src_ref=ref, dst_ref=ref, send_sem=c_send, recv_sem=sem, device_id=other, device_id_type=MESH
        ).start()

    def pass_on(dz, s, steps):
        ref = gath.at[(z + nz - dz) % nz, c, s]
        wait(ref, g_recv.at[dz, s])
        for step in steps:
            pltpu.make_async_remote_copy(
                src_ref=ref, dst_ref=ref, send_sem=r_send, recv_sem=g_recv.at[(dz + step) % nz, s],
                device_id=(2 * ((z + nz + step) % nz) + c, t), device_id_type=MESH,
            ).start()
        hand(ref, c_recv.at[dz, s])

    wait(ov.at[(x + 1) % NX, low], o_recv.at[0])
    turn(((x + 1) % NX, low, 4, left))
    wait(ov.at[(x + NX - 1) % NX, high], o_recv.at[1])
    turn(((x + NX - 1) % NX, high, 5, right))

    far = nz // 2
    pass_on(2, 0, (1, 2))
    pass_on(nz - 2, 1, (-1, -2))
    pass_on(2, 1, (1,))
    pass_on(nz - 2, 0, (-1,))
    for dz in (1, nz - 1):
        for s in range(slots):
            pass_on(dz, s, ())
    for f in range(2):
        @pl.when(jnp.logical_not(jnp.logical_and(alone, f == c)))
        def _():
            wait(gath.at[z, c, :, f], near_recv.at[f])
    for s in range(slots):
        hand(gath.at[z, c, s], c_recv.at[0, s])

    def project(batch):
        origins = [(z + nz - dz) % nz for dz in batch]
        for dz, origin in zip(batch, origins):
            for s in range(slots):
                wait(gath.at[origin, 1 - c, s], c_recv.at[dz, s])
        product = None
        for source in range(NX):
            rows = [gath[o, source % 2, s, source // 2] for o in origins for s in range(slots)]
            term = lax.dot_general(
                jnp.concatenate(rows, axis=0), ov[source], (((1,), (1,)), ((), ())), preferred_element_type=F32
            )
            product = term if product is None else product + term
        for i, (dz, origin) in enumerate(zip(batch, origins)):
            piece = product[i * rows_out:(i + 1) * rows_out]
            ysnd[dz] = piece.astype(BF16)

            @pl.when(origin != y)
            def _():
                pltpu.make_async_remote_copy(
                    src_ref=ysnd.at[dz], dst_ref=yrcv.at[y], send_sem=y_send, recv_sem=y_recv,
                    device_id=(d, origin * NX + x), device_id_type=MESH,
                ).start()

            @pl.when(origin == y)
            def _():
                acc[...] = piece
                yrcv[y] = jnp.zeros_like(ysnd[dz])

    for dz in (3, nz - 3, far):
        for s in range(slots):
            pass_on(dz, s, ())
    for owner, rows, sem in ((x + 1, high, 2), (x + NX - 1, low, 3), (x + 2, low, 4), (x + 2, high, 5)):
        wait(ov.at[owner % NX, rows], o_recv.at[sem])
    project((0, 1, nz - 1, 2, nz - 2))
    project((3, nz - 3, far))

    wait(yrcv.at[pl.ds(0, nz - 1)], y_recv)
    total = residual + acc[...]
    for i in range(nz):
        total += yrcv[i].astype(F32)
    back = one_hot(rows_out, rows_out, lambda r: (r % slots) * part + r // slots)
    out_ref[...] = dot(back, total.astype(BF16)).astype(BF16)

    wait(snd.at[pl.ds(0, nt - 1)], a_send)
    wait(ov.at[pl.ds(0, NX - 1)], o_send)
    for dz in direct[:-1]:
        wait(vals, g_send.at[dz])
    for e in range(2):
        @pl.when(jnp.logical_not(jnp.logical_and(alone, x % 2 == e)))
        def _():
            wait(gath.at[0, 0, 0], near_send.at[e])
    wait(gath.at[pl.ds(0, 3), 0], r_send)
    wait(gath.at[:, 0], c_send)
    wait(ysnd.at[pl.ds(0, nz - 1)], y_send)


def body(queries, latent_cache, lengths, counts, value_up, out_proj, residual, nd, nt):
    queries, latent_cache, out_proj = queries.swapaxes(1, 2), latent_cache.swapaxes(1, 2), out_proj.T
    slots, _, heads = queries.shape
    local, latent, width = value_up.shape
    nz = nd // 2
    rows, columns = residual.shape
    part = rows // slots
    block = local * latent // LANES
    any_spec = pl.BlockSpec(memory_space=pl.ANY)
    vmem, dma = pltpu.VMEM, pltpu.SemaphoreType.DMA
    return pl.pallas_call(
        functools.partial(kernel, nd, nt),
        out_shape=jax.ShapeDtypeStruct((rows, columns), BF16),
        in_specs=[any_spec] * 7,
        out_specs=pl.BlockSpec(memory_space=pltpu.VMEM),
        scratch_shapes=[
            pltpu.SMEM(lengths.shape, jnp.int32),
            pltpu.SMEM(counts.shape, jnp.int32),
            vmem(queries.shape, BF16),
            vmem(latent_cache.shape, BF16),
            vmem(value_up.shape, BF16),
            vmem((NX,) + out_proj.shape, BF16),
            vmem(residual.shape, BF16),
            vmem((nt * block, nt * block), BF16),
            vmem((nt * block, nt * block), BF16),
            vmem((nt, slots, block, LANES), BF16),
            vmem((nt, slots, block, LANES), BF16),
            vmem((slots, 2, part, local * width), BF16),
            vmem((nz, 2, slots, 2, part, local * width), BF16),
            vmem((nz, rows, columns), BF16),
            vmem((nz, rows, columns), BF16),
            vmem((rows, columns), F32),
            dma((9,)), dma, dma, dma, dma((6,)), dma((nz,)), dma((nz, slots)), dma((2,)), dma((2,)),
            dma, dma, dma((nz, slots)), dma, dma,
        ],
        compiler_params=pltpu.CompilerParams(
            collective_id=0, has_side_effects=True, vmem_limit_bytes=VMEM_LIMIT
        ),
        name="decode_attention",
    )(lengths, counts, queries, latent_cache, value_up, out_proj, residual)


def solution(mesh):
    in_specs = (
        P(("dp", "tp"), None, None),
        P(("dp", "tp"), None, None),
        P(("dp", "tp")),
        P(("dp", "tp")),
        P("tp", None, None),
        P("tp", "dp"),
        P("tp", "dp"),
    )
    step = functools.partial(body, nd=mesh.shape["dp"], nt=mesh.shape["tp"])
    return jax.shard_map(step, mesh=mesh, in_specs=in_specs, out_specs=P("tp", "dp"), check_vma=False)
```

```python
import functools
import math

import jax
import jax.numpy as jnp
from jax import lax
from jax.experimental import pallas as pl
from jax.experimental.pallas import tpu as pltpu
from jax.sharding import PartitionSpec as P

MESH = pl.DeviceIdType.MESH
LANES = 128
NX = 4
VMEM_LIMIT = 55168 * 1024
SCALE = 192.0 ** (-0.5)
F32 = jnp.float32
BF16 = jnp.bfloat16


def one_hot(rows, cols, column_of_row):
    row = lax.broadcasted_iota(jnp.int32, (rows, cols), 0)
    col = lax.broadcasted_iota(jnp.int32, (rows, cols), 1)
    return (col == column_of_row(row)).astype(F32).astype(BF16)


def outward(n):
    return sorted(range(n), key=lambda step: (-min(step, n - step), step))


def dot(a, b):
    return jnp.dot(a, b, preferred_element_type=F32)


def kernel(
    nd, nt, len_hbm, cnt_hbm, q_hbm, c_hbm, w_hbm, o_hbm, r_hbm, out_ref,
    len_ref, cnt_ref, qv, cv, wv, ov, rv, owner_map, head_map, snd, rcv, vals, gath, ysnd, yrcv, acc,
    load_sem, a_send, a_recv, o_send, o_recv, g_send, g_recv, near_send, near_recv, r_send, c_send, c_recv, y_send, y_recv,
):
    nz = nd // 2
    d, t = lax.axis_index("dp"), lax.axis_index("tp")
    z, c = lax.div(d, 2), lax.rem(d, 2)
    y, x = lax.div(t, NX), lax.rem(t, NX)
    other = (2 * z + 1 - c, t)
    alone = x == 3 * c
    slots = q_hbm.shape[0]
    heads = q_hbm.shape[2]
    local, latent, width = w_hbm.shape
    pieces = latent // LANES
    block = local * pieces
    rows_out, columns = out_ref.shape
    part = rows_out // slots
    direct = (2, nz - 2, 1, nz - 1, 0)

    def load(i, src, dst):
        return pltpu.make_async_copy(src, dst, load_sem.at[i])

    loads = [(load(2 * s, q_hbm.at[s], qv.at[s]), load(2 * s + 1, c_hbm.at[s], cv.at[s])) for s in range(slots)]
    late = [load(4, w_hbm, wv), load(5, o_hbm, ov.at[x]), load(6, r_hbm, rv)]
    loads[0] += (load(7, len_hbm, len_ref), load(8, cnt_hbm, cnt_ref))
    for copy in loads[0]:
        copy.start()

    barrier = pltpu.get_barrier_semaphore()

    def greet(device):
        pl.semaphore_signal(barrier, inc=1, device_id=device, device_id_type=MESH)

    ny = nt // NX
    row = [lax.rem(y + step, ny) * NX for step in outward(ny)]
    column = [lax.rem(x + step, NX) for step in outward(NX)]
    peers = [r + q for r in row for q in column][:-1]
    for peer in peers:
        greet((d, peer))
    greet(other)
    for dz in direct[:-1]:
        greet((2 * ((z + dz) % nz) + c, t))
    for dz in direct:
        for f in range(2):
            source = (2 * ((z + nz - dz) % nz) + x // 2, y * NX + c + 2 * f)
            if dz == 0:
                @pl.when(jnp.logical_not(jnp.logical_and(alone, f == c)))
                def _():
                    greet(source)
            else:
                greet(source)

    owner_map[...] = one_hot(
        heads * pieces, heads * pieces,
        lambda r: ((r // local) % pieces) * heads + (r // block) * local + r % local,
    )
    for s in range(slots):
        for copy in loads[s]:
            copy.wait()
        for copy in loads[s + 1] if s + 1 < slots else late:
            copy.start()
        scores = lax.dot_general(qv[s], cv[s], (((0,), (0,)), ((), ())), preferred_element_type=F32)
        position = lax.broadcasted_iota(jnp.int32, scores.shape, 1)
        scores = jnp.where(position < len_ref[s], scores, -jnp.inf)
        top = jnp.max(scores, axis=1, keepdims=True)
        weight = jnp.exp2((scores - top) * (SCALE * math.log2(math.e)))
        weight = (weight * (1.0 / jnp.sum(weight, axis=1, keepdims=True))).astype(BF16)
        attended = lax.dot_general(weight, cv[s, :latent], (((1,), (1,)), ((), ())), preferred_element_type=F32)
        attended = jnp.where(cnt_ref[0] > s, attended, 0.0).astype(BF16)
        stacked = jnp.concatenate([attended[:, k * LANES:(k + 1) * LANES] for k in range(pieces)], axis=0)
        snd[:, s] = dot(owner_map[...], stacked).astype(BF16).reshape(nt, block, LANES)
    pl.semaphore_wait(barrier, nt + 3 * len(direct) - 1 - alone.astype(jnp.int32))

    for copy in late:
        copy.wait()

    low, high = pl.ds(0, columns // 2), pl.ds(columns // 2, columns // 2)
    left, right = (d, y * NX + (x + NX - 1) % NX), (d, y * NX + (x + 1) % NX)

    def turn(*moves, starts=range(0, columns // 2, 32)):
        for start in starts:
            for owner, rows, sem, device in moves:
                ref = ov.at[owner, pl.ds(rows.start + start, 32)]
                pltpu.make_async_remote_copy(
                    src_ref=ref, dst_ref=ref, send_sem=o_send, recv_sem=o_recv.at[sem],
                    device_id=device, device_id_type=MESH,
                ).start()

    def scatter(first, last):
        for to in peers[first:last]:
            pltpu.make_async_remote_copy(
                src_ref=snd.at[to], dst_ref=rcv.at[t], send_sem=a_send, recv_sem=a_recv,
                device_id=(d, to), device_id_type=MESH,
            ).start()

    scatter(0, 16)
    for n, start in enumerate(range(0, columns // 2, 32)):
        scatter(16 + 2 * n, 16 + 2 * n + 2)
        turn((x, low, 0, left), (x, high, 1, right), starts=(start,))
    scatter(16 + columns // 32, nt - 1)
    rcv[t] = snd[t]

    head_map[...] = one_hot(nt * block, nt * block, lambda r: (r % nt) * block + r // nt)
    turn((x, high, 2, left), (x, low, 3, right))
    residual = dot(one_hot(rows_out, rows_out, lambda r: (r % part) * slots + r // part), rv[...])

    def wait(ref, sem):
        pltpu.make_async_copy(ref, ref, sem).wait()

    wait(rcv.at[pl.ds(0, nt - 1)], a_recv)
    arrived = jnp.concatenate([rcv[:, s].reshape(nt * block, LANES) for s in range(slots)], axis=1)
    arrived = dot(head_map[...], arrived).astype(BF16)
    values = []
    for h in range(local):
        rows = []
        for s in range(slots):
            starts = [(k * local + h) * nt for k in range(pieces)]
            rows.append(jnp.concatenate([arrived[a:a + nt, s * LANES:(s + 1) * LANES] for a in starts], axis=1))
        values.append(dot(jnp.concatenate(rows, axis=0), wv[h]).astype(BF16))
    vals[...] = jnp.concatenate(values, axis=1).reshape(slots, 2, part, local * width)

    def spread(dz, s):
        for e in range(2):
            copy = pltpu.make_async_remote_copy(
                src_ref=vals.at[s, e], dst_ref=gath.at[z, x % 2, s, x // 2],
                send_sem=g_send.at[dz] if dz else near_send.at[e],
                recv_sem=g_recv.at[dz, s] if dz else near_recv.at[x // 2],
                device_id=(2 * ((z + dz) % nz) + x % 2, y * NX + 2 * c + e), device_id_type=MESH,
            )
            if dz:
                copy.start()
            else:
                @pl.when(jnp.logical_not(jnp.logical_and(alone, x % 2 == e)))
                def _():
                    copy.start()

    for dz, s in ((2, 0), (nz - 2, 1), (2, 1), (nz - 2, 0)):
        spread(dz, s)
    for dz in (0, 1, nz - 1):
        for s in range(slots):
            spread(dz, s)

    for s in range(slots):
        @pl.when(alone)
        def _():
            gath[z, c, s, x // 2] = vals[s, x % 2]

    def hand(ref, sem):
        pltpu.make_async_remote_copy(
            src_ref=ref, dst_ref=ref, send_sem=c_send, recv_sem=sem, device_id=other, device_id_type=MESH
        ).start()

    def pass_on(dz, s, steps):
        ref = gath.at[(z + nz - dz) % nz, c, s]
        wait(ref, g_recv.at[dz, s])
        for step in steps:
            pltpu.make_async_remote_copy(
                src_ref=ref, dst_ref=ref, send_sem=r_send, recv_sem=g_recv.at[(dz + step) % nz, s],
                device_id=(2 * ((z + nz + step) % nz) + c, t), device_id_type=MESH,
            ).start()
        hand(ref, c_recv.at[dz, s])

    wait(ov.at[(x + 1) % NX, low], o_recv.at[0])
    turn(((x + 1) % NX, low, 4, left))
    wait(ov.at[(x + NX - 1) % NX, high], o_recv.at[1])
    turn(((x + NX - 1) % NX, high, 5, right))

    far = nz // 2
    pass_on(2, 0, (1, 2))
    pass_on(nz - 2, 1, (-1, -2))
    pass_on(2, 1, (1,))
    pass_on(nz - 2, 0, (-1,))
    for dz in (1, nz - 1):
        for s in range(slots):
            pass_on(dz, s, ())
    for f in range(2):
        @pl.when(jnp.logical_not(jnp.logical_and(alone, f == c)))
        def _():
            wait(gath.at[z, c, :, f], near_recv.at[f])
    for s in range(slots):
        hand(gath.at[z, c, s], c_recv.at[0, s])

    def project(batch):
        origins = [(z + nz - dz) % nz for dz in batch]
        for dz, origin in zip(batch, origins):
            for s in range(slots):
                wait(gath.at[origin, 1 - c, s], c_recv.at[dz, s])
        product = None
        for source in range(NX):
            rows = [gath[o, source % 2, s, source // 2] for o in origins for s in range(slots)]
            term = lax.dot_general(
                jnp.concatenate(rows, axis=0), ov[source], (((1,), (1,)), ((), ())), preferred_element_type=F32
            )
            product = term if product is None else product + term
        for i, (dz, origin) in enumerate(zip(batch, origins)):
            piece = product[i * rows_out:(i + 1) * rows_out]
            ysnd[dz] = piece.astype(BF16)

            @pl.when(origin != y)
            def _():
                pltpu.make_async_remote_copy(
                    src_ref=ysnd.at[dz], dst_ref=yrcv.at[y], send_sem=y_send, recv_sem=y_recv,
                    device_id=(d, origin * NX + x), device_id_type=MESH,
                ).start()

            @pl.when(origin == y)
            def _():
                acc[...] = piece
                yrcv[y] = jnp.zeros_like(ysnd[dz])

    for dz in (3, nz - 3, far):
        for s in range(slots):
            pass_on(dz, s, ())
    for owner, rows, sem in ((x + 1, high, 2), (x + NX - 1, low, 3), (x + 2, low, 4), (x + 2, high, 5)):
        wait(ov.at[owner % NX, rows], o_recv.at[sem])
    project((0, 1, nz - 1, 2, nz - 2))
    project((3, nz - 3, far))

    wait(yrcv.at[pl.ds(0, nz - 1)], y_recv)
    total = residual + acc[...]
    for i in range(nz):
        total += yrcv[i].astype(F32)
    back = one_hot(rows_out, rows_out, lambda r: (r % slots) * part + r // slots)
    out_ref[...] = dot(back, total.astype(BF16)).astype(BF16)

    wait(snd.at[pl.ds(0, nt - 1)], a_send)
    wait(ov.at[pl.ds(0, NX - 1)], o_send)
    for dz in direct[:-1]:
        wait(vals, g_send.at[dz])
    for e in range(2):
        @pl.when(jnp.logical_not(jnp.logical_and(alone, x % 2 == e)))
        def _():
            wait(gath.at[0, 0, 0], near_send.at[e])
    wait(gath.at[pl.ds(0, 3), 0], r_send)
    wait(gath.at[:, 0], c_send)
    wait(ysnd.at[pl.ds(0, nz - 1)], y_send)


def body(queries, latent_cache, lengths, counts, value_up, out_proj, residual, nd, nt):
    queries, latent_cache, out_proj = queries.swapaxes(1, 2), latent_cache.swapaxes(1, 2), out_proj.T
    slots, _, heads = queries.shape
    local, latent, width = value_up.shape
    nz = nd // 2
    rows, columns = residual.shape
    part = rows // slots
    block = local * latent // LANES
    any_spec = pl.BlockSpec(memory_space=pl.ANY)
    vmem, dma = pltpu.VMEM, pltpu.SemaphoreType.DMA
    return pl.pallas_call(
        functools.partial(kernel, nd, nt),
        out_shape=jax.ShapeDtypeStruct((rows, columns), BF16),
        in_specs=[any_spec] * 7,
        out_specs=pl.BlockSpec(memory_space=pltpu.VMEM),
        scratch_shapes=[
            pltpu.SMEM(lengths.shape, jnp.int32),
            pltpu.SMEM(counts.shape, jnp.int32),
            vmem(queries.shape, BF16),
            vmem(latent_cache.shape, BF16),
            vmem(value_up.shape, BF16),
            vmem((NX,) + out_proj.shape, BF16),
            vmem(residual.shape, BF16),
            vmem((nt * block, nt * block), BF16),
            vmem((nt * block, nt * block), BF16),
            vmem((nt, slots, block, LANES), BF16),
            vmem((nt, slots, block, LANES), BF16),
            vmem((slots, 2, part, local * width), BF16),
            vmem((nz, 2, slots, 2, part, local * width), BF16),
            vmem((nz, rows, columns), BF16),
            vmem((nz, rows, columns), BF16),
            vmem((rows, columns), F32),
            dma((9,)), dma, dma, dma, dma((6,)), dma((nz,)), dma((nz, slots)), dma((2,)), dma((2,)),
            dma, dma, dma((nz, slots)), dma, dma,
        ],
        compiler_params=pltpu.CompilerParams(
            collective_id=0, has_side_effects=True, vmem_limit_bytes=VMEM_LIMIT
        ),
        name="decode_attention",
    )(lengths, counts, queries, latent_cache, value_up, out_proj, residual)


def solution(mesh):
    in_specs = (
        P(("dp", "tp"), None, None),
        P(("dp", "tp"), None, None),
        P(("dp", "tp")),
        P(("dp", "tp")),
        P("tp", None, None),
        P("tp", "dp"),
        P("tp", "dp"),
    )
    step = functools.partial(body, nd=mesh.shape["dp"], nt=mesh.shape["tp"])
    return jax.shard_map(step, mesh=mesh, in_specs=in_specs, out_specs=P("tp", "dp"), check_vma=False)
```

```python
import functools
import math

import jax
import jax.numpy as jnp
from jax import lax
from jax.experimental import pallas as pl
from jax.experimental.pallas import tpu as pltpu
from jax.sharding import PartitionSpec as P

MESH = pl.DeviceIdType.MESH
LANES = 128
NX = 4
VMEM_LIMIT = 55168 * 1024
SCALE = 192.0 ** (-0.5)
F32 = jnp.float32
BF16 = jnp.bfloat16


def one_hot(rows, cols, column_of_row):
    row = lax.broadcasted_iota(jnp.int32, (rows, cols), 0)
    col = lax.broadcasted_iota(jnp.int32, (rows, cols), 1)
    return (col == column_of_row(row)).astype(F32).astype(BF16)


def outward(n):
    return sorted(range(n), key=lambda step: (-min(step, n - step), step))


def dot(a, b):
    return jnp.dot(a, b, preferred_element_type=F32)


def kernel(
    nd, nt, len_hbm, cnt_hbm, q_hbm, c_hbm, w_hbm, o_hbm, r_hbm, out_ref,
    len_ref, cnt_ref, qv, cv, wv, ov, rv, owner_map, head_map, snd, rcv, vals, gath, ysnd, yrcv, acc,
    load_sem, a_send, a_recv, o_send, o_recv, g_send, g_recv, near_send, near_recv, r_send, c_send, c_recv, y_send, y_recv,
):
    nz = nd // 2
    d, t = lax.axis_index("dp"), lax.axis_index("tp")
    z, c = lax.div(d, 2), lax.rem(d, 2)
    y, x = lax.div(t, NX), lax.rem(t, NX)
    other = (2 * z + 1 - c, t)
    alone = x == 3 * c
    slots = q_hbm.shape[0]
    heads = q_hbm.shape[2]
    local, latent, width = w_hbm.shape
    pieces = latent // LANES
    block = local * pieces
    rows_out, columns = out_ref.shape
    part = rows_out // slots
    direct = (2, nz - 2, 1, nz - 1, 0)

    def load(i, src, dst):
        return pltpu.make_async_copy(src, dst, load_sem.at[i])

    quarter = c_hbm.shape[1] // 4
    loads = []
    for s in range(slots):
        loads.append([load(9 + s, q_hbm.at[s], qv.at[s])])
        for i in range(4):
            rows = pl.ds(i * quarter, quarter)
            loads[s].append(load(4 * s + i, c_hbm.at[s, rows], cv.at[s, rows]))
    late = [load(11, w_hbm, wv), load(12, o_hbm, ov.at[x]), load(13, r_hbm, rv)]
    loads[0] += [load(8, len_hbm, len_ref), load(14, cnt_hbm, cnt_ref)]
    for copy in loads[0]:
        copy.start()

    barrier = pltpu.get_barrier_semaphore()

    def greet(device):
        pl.semaphore_signal(barrier, inc=1, device_id=device, device_id_type=MESH)

    ny = nt // NX
    row = [lax.rem(y + step, ny) * NX for step in outward(ny)]
    column = [lax.rem(x + step, NX) for step in outward(NX)]
    peers = [r + q for r in row for q in column][:-1]
    for peer in peers:
        greet((d, peer))
    greet(other)
    for dz in direct[:-1]:
        greet((2 * ((z + dz) % nz) + c, t))
    for dz in direct:
        for f in range(2):
            source = (2 * ((z + nz - dz) % nz) + x // 2, y * NX + c + 2 * f)
            if dz == 0:
                @pl.when(jnp.logical_not(jnp.logical_and(alone, f == c)))
                def _():
                    greet(source)
            else:
                greet(source)

    owner_map[...] = one_hot(
        heads * pieces, heads * pieces,
        lambda r: ((r // local) % pieces) * heads + (r // block) * local + r % local,
    )
    for s in range(slots):
        for copy in loads[s]:
            copy.wait()
        for copy in loads[s + 1] if s + 1 < slots else late:
            copy.start()
        scores = lax.dot_general(qv[s], cv[s], (((0,), (0,)), ((), ())), preferred_element_type=F32)
        position = lax.broadcasted_iota(jnp.int32, scores.shape, 1)
        scores = jnp.where(position < len_ref[s], scores, -jnp.inf)
        top = jnp.max(scores, axis=1, keepdims=True)
        weight = jnp.exp2((scores - top) * (SCALE * math.log2(math.e)))
        weight = (weight * (1.0 / jnp.sum(weight, axis=1, keepdims=True))).astype(BF16)
        attended = lax.dot_general(weight, cv[s, :latent], (((1,), (1,)), ((), ())), preferred_element_type=F32)
        attended = jnp.where(cnt_ref[0] > s, attended, 0.0).astype(BF16)
        stacked = jnp.concatenate([attended[:, k * LANES:(k + 1) * LANES] for k in range(pieces)], axis=0)
        snd[:, s] = dot(owner_map[...], stacked).astype(BF16).reshape(nt, block, LANES)
    pl.semaphore_wait(barrier, nt + 3 * len(direct) - 1 - alone.astype(jnp.int32))

    for copy in late:
        copy.wait()

    low, high = pl.ds(0, columns // 2), pl.ds(columns // 2, columns // 2)
    left, right = (d, y * NX + (x + NX - 1) % NX), (d, y * NX + (x + 1) % NX)

    def turn(*moves, starts=range(0, columns // 2, 32)):
        for start in starts:
            for owner, rows, sem, device in moves:
                ref = ov.at[owner, pl.ds(rows.start + start, 32)]
                pltpu.make_async_remote_copy(
                    src_ref=ref, dst_ref=ref, send_sem=o_send, recv_sem=o_recv.at[sem],
                    device_id=device, device_id_type=MESH,
                ).start()

    def scatter(first, last):
        for to in peers[first:last]:
            pltpu.make_async_remote_copy(
                src_ref=snd.at[to], dst_ref=rcv.at[t], send_sem=a_send, recv_sem=a_recv,
                device_id=(d, to), device_id_type=MESH,
            ).start()

    scatter(0, 16)
    for n, start in enumerate(range(0, columns // 2, 32)):
        scatter(16 + 2 * n, 16 + 2 * n + 2)
        turn((x, low, 0, left), (x, high, 1, right), starts=(start,))
    scatter(16 + columns // 32, nt - 1)
    rcv[t] = snd[t]

    head_map[...] = one_hot(nt * block, nt * block, lambda r: (r % nt) * block + r // nt)
    turn((x, high, 2, left), (x, low, 3, right))
    residual = dot(one_hot(rows_out, rows_out, lambda r: (r % part) * slots + r // part), rv[...])

    def wait(ref, sem):
        pltpu.make_async_copy(ref, ref, sem).wait()

    wait(rcv.at[pl.ds(0, nt - 1)], a_recv)
    arrived = jnp.concatenate([rcv[:, s].reshape(nt * block, LANES) for s in range(slots)], axis=1)
    arrived = dot(head_map[...], arrived).astype(BF16)
    values = []
    for h in range(local):
        rows = []
        for s in range(slots):
            starts = [(k * local + h) * nt for k in range(pieces)]
            rows.append(jnp.concatenate([arrived[a:a + nt, s * LANES:(s + 1) * LANES] for a in starts], axis=1))
        values.append(dot(jnp.concatenate(rows, axis=0), wv[h]).astype(BF16))
    vals[...] = jnp.concatenate(values, axis=1).reshape(slots, 2, part, local * width)

    def spread(dz, s):
        for e in range(2):
            copy = pltpu.make_async_remote_copy(
                src_ref=vals.at[s, e], dst_ref=gath.at[z, x % 2, s, x // 2],
                send_sem=g_send.at[dz] if dz else near_send.at[e],
                recv_sem=g_recv.at[dz, s] if dz else near_recv.at[x // 2],
                device_id=(2 * ((z + dz) % nz) + x % 2, y * NX + 2 * c + e), device_id_type=MESH,
            )
            if dz:
                copy.start()
            else:
                @pl.when(jnp.logical_not(jnp.logical_and(alone, x % 2 == e)))
                def _():
                    copy.start()

    for dz, s in ((2, 0), (nz - 2, 1), (2, 1), (nz - 2, 0)):
        spread(dz, s)
    for dz in (0, 1, nz - 1):
        for s in range(slots):
            spread(dz, s)

    for s in range(slots):
        @pl.when(alone)
        def _():
            gath[z, c, s, x // 2] = vals[s, x % 2]

    def hand(ref, sem):
        pltpu.make_async_remote_copy(
            src_ref=ref, dst_ref=ref, send_sem=c_send, recv_sem=sem, device_id=other, device_id_type=MESH
        ).start()

    def pass_on(dz, s, steps):
        ref = gath.at[(z + nz - dz) % nz, c, s]
        wait(ref, g_recv.at[dz, s])
        for step in steps:
            pltpu.make_async_remote_copy(
                src_ref=ref, dst_ref=ref, send_sem=r_send, recv_sem=g_recv.at[(dz + step) % nz, s],
                device_id=(2 * ((z + nz + step) % nz) + c, t), device_id_type=MESH,
            ).start()
        hand(ref, c_recv.at[dz, s])

    wait(ov.at[(x + 1) % NX, low], o_recv.at[0])
    turn(((x + 1) % NX, low, 4, left))
    wait(ov.at[(x + NX - 1) % NX, high], o_recv.at[1])
    turn(((x + NX - 1) % NX, high, 5, right))

    far = nz // 2
    pass_on(2, 0, (1, 2))
    pass_on(nz - 2, 1, (-1, -2))
    pass_on(2, 1, (1,))
    pass_on(nz - 2, 0, (-1,))
    for dz in (1, nz - 1):
        for s in range(slots):
            pass_on(dz, s, ())
    for f in range(2):
        @pl.when(jnp.logical_not(jnp.logical_and(alone, f == c)))
        def _():
            wait(gath.at[z, c, :, f], near_recv.at[f])
    for s in range(slots):
        hand(gath.at[z, c, s], c_recv.at[0, s])

    def project(batch):
        origins = [(z + nz - dz) % nz for dz in batch]
        for dz, origin in zip(batch, origins):
            for s in range(slots):
                wait(gath.at[origin, 1 - c, s], c_recv.at[dz, s])
        product = None
        for source in range(NX):
            rows = [gath[o, source % 2, s, source // 2] for o in origins for s in range(slots)]
            term = lax.dot_general(
                jnp.concatenate(rows, axis=0), ov[source], (((1,), (1,)), ((), ())), preferred_element_type=F32
            )
            product = term if product is None else product + term
        for i, (dz, origin) in enumerate(zip(batch, origins)):
            piece = product[i * rows_out:(i + 1) * rows_out]
            ysnd[dz] = piece.astype(BF16)

            @pl.when(origin != y)
            def _():
                pltpu.make_async_remote_copy(
                    src_ref=ysnd.at[dz], dst_ref=yrcv.at[y], send_sem=y_send, recv_sem=y_recv,
                    device_id=(d, origin * NX + x), device_id_type=MESH,
                ).start()

            @pl.when(origin == y)
            def _():
                acc[...] = piece
                yrcv[y] = jnp.zeros_like(ysnd[dz])

    for dz in (3, nz - 3, far):
        for s in range(slots):
            pass_on(dz, s, ())
    for owner, rows, sem in ((x + 1, high, 2), (x + NX - 1, low, 3), (x + 2, low, 4), (x + 2, high, 5)):
        wait(ov.at[owner % NX, rows], o_recv.at[sem])
    project((0, 1, nz - 1, 2, nz - 2))
    project((3, nz - 3, far))

    wait(yrcv.at[pl.ds(0, nz - 1)], y_recv)
    total = residual + acc[...]
    for i in range(nz):
        total += yrcv[i].astype(F32)
    back = one_hot(rows_out, rows_out, lambda r: (r % slots) * part + r // slots)
    out_ref[...] = dot(back, total.astype(BF16)).astype(BF16)

    wait(snd.at[pl.ds(0, nt - 1)], a_send)
    wait(ov.at[pl.ds(0, NX - 1)], o_send)
    for dz in direct[:-1]:
        wait(vals, g_send.at[dz])
    for e in range(2):
        @pl.when(jnp.logical_not(jnp.logical_and(alone, x % 2 == e)))
        def _():
            wait(gath.at[0, 0, 0], near_send.at[e])
    wait(gath.at[pl.ds(0, 3), 0], r_send)
    wait(gath.at[:, 0], c_send)
    wait(ysnd.at[pl.ds(0, nz - 1)], y_send)


def body(queries, latent_cache, lengths, counts, value_up, out_proj, residual, nd, nt):
    queries, latent_cache, out_proj = queries.swapaxes(1, 2), latent_cache.swapaxes(1, 2), out_proj.T
    slots, _, heads = queries.shape
    local, latent, width = value_up.shape
    nz = nd // 2
    rows, columns = residual.shape
    part = rows // slots
    block = local * latent // LANES
    any_spec = pl.BlockSpec(memory_space=pl.ANY)
    vmem, dma = pltpu.VMEM, pltpu.SemaphoreType.DMA
    return pl.pallas_call(
        functools.partial(kernel, nd, nt),
        out_shape=jax.ShapeDtypeStruct((rows, columns), BF16),
        in_specs=[any_spec] * 7,
        out_specs=pl.BlockSpec(memory_space=pltpu.VMEM),
        scratch_shapes=[
            pltpu.SMEM(lengths.shape, jnp.int32),
            pltpu.SMEM(counts.shape, jnp.int32),
            vmem(queries.shape, BF16),
            vmem(latent_cache.shape, BF16),
            vmem(value_up.shape, BF16),
            vmem((NX,) + out_proj.shape, BF16),
            vmem(residual.shape, BF16),
            vmem((nt * block, nt * block), BF16),
            vmem((nt * block, nt * block), BF16),
            vmem((nt, slots, block, LANES), BF16),
            vmem((nt, slots, block, LANES), BF16),
            vmem((slots, 2, part, local * width), BF16),
            vmem((nz, 2, slots, 2, part, local * width), BF16),
            vmem((nz, rows, columns), BF16),
            vmem((nz, rows, columns), BF16),
            vmem((rows, columns), F32),
            dma((15,)), dma, dma, dma, dma((6,)), dma((nz,)), dma((nz, slots)), dma((2,)), dma((2,)),
            dma, dma, dma((nz, slots)), dma, dma,
        ],
        compiler_params=pltpu.CompilerParams(
            collective_id=0, has_side_effects=True, vmem_limit_bytes=VMEM_LIMIT
        ),
        name="decode_attention",
    )(lengths, counts, queries, latent_cache, value_up, out_proj, residual)


def solution(mesh):
    in_specs = (
        P(("dp", "tp"), None, None),
        P(("dp", "tp"), None, None),
        P(("dp", "tp")),
        P(("dp", "tp")),
        P("tp", None, None),
        P("tp", "dp"),
        P("tp", "dp"),
    )
    step = functools.partial(body, nd=mesh.shape["dp"], nt=mesh.shape["tp"])
    return jax.shard_map(step, mesh=mesh, in_specs=in_specs, out_specs=P("tp", "dp"), check_vma=False)
```
